32 devices in a mesh: groups: 2 (over y), patch: 4 (over z), band: 2 (over x), width: 2 (over core).
Axes of the slice: x: 2, y: 2, z: 4, core: 2. Of those that a mesh axis runs over, the one named last changes fastest.
Arguments:
- grid_latent: bfloat16 [8192, 384], P(('groups', 'patch', 'band', 'width')), parts along dimension 0, may hold values from -6 to 6
- mesh_latent: bfloat16 [64, 32, 384], P(('groups', 'patch'), ('band', 'width')), parts along dimension 0, may hold values from -6 to 6
- w_first: bfloat16 [5, 768, 384], P(None, None, 'width'), may hold values from -0.21875 to 0.21875
- first_bias: float32 [5, 384], replicated, may hold values from -4 to 4
- w_second: bfloat16 [5, 384, 384], P(None, None, 'width'), may hold values from -0.3125 to 0.3125
- norm_gain: float32 [5, 384], replicated, may hold values from 0.5 to 1.5
- encode_source: int32 [4, 4, 512], P('patch', ('band', 'width')), may hold values from 0 to 255, as said below
- encode_target: int32 [4, 4, 512], P('patch', ('band', 'width')), may hold values from 100 to 475, as said below
- encode_count: int32 [4, 4], P('patch', ('band', 'width')), may hold values from 256 to 512
- mesh_sender: int32 [4, 4, 512], P('patch', ('band', 'width')), may hold values from 0 to 575, as said below
- mesh_receiver: int32 [4, 4, 512], P('patch', ('band', 'width')), may hold values from 0 to 63
- decode_source: int32 [4, 4, 256, 3], P('patch', ('band', 'width')), may hold values from 175 to 400, as said below
Outputs:
- grid_out: bfloat16 [8192, 384], P(('groups', 'patch', 'band', 'width')), parts along dimension 0
- mesh_out: bfloat16 [64, 32, 384], P(('groups', 'patch'), ('band', 'width')), parts along dimension 0
The draws below stay inside these ranges and needn't reach their ends.
There are 2 independent parts, one for each index of `groups`. The reference program is written for one: setup_inputs(seed, part) draws one part's arguments, and reference() takes and returns one part's arrays. A program takes and returns all parts, laid end to end along the dimension named above; an argument that names none is the same for every part. Nothing has to cross between parts.
Inputs may be any that keep to these rules, and one draw needn't show every extreme that they name: `encode_source`: slot e < 256 holds e. `encode_target`: row and column of the extended index lie within 4 cells of the device's own block. `mesh_sender`: row and column lie in the 3 x 3 neighbourhood of blocks around the receiving block. `decode_source`: row and column of the extended index lie within one cell of the device's own block.
All inputs are finite; a program needn't handle non-finite values.
Results may differ from the reference program's by a relative error of at most 0.0095.
Values may be sent and summed in bfloat16 or wider, within the bound.
A program may use at most 64 MiB of HBM per device.

```python
import jax
import jax.numpy as jnp
from jax import lax

D = 384
GRID_DEV = 256
MSIDE = 8
DEC_DEGREE = 3
MESH_DEV = 64
EDGE_DEV = 512
ENC_CAP = 512
REACH = 4
SECTORS = 4
NGRID = 4096
NX = 32
NY = 32
N_PATCH = 4


def near_spot(key_in, place_shape, offset_shape, spread):
    key_row, key_col, key_drow, key_dcol = jax.random.split(key_in, 4)
    place_row = jax.random.randint(key_row, place_shape, 0, MSIDE)
    place_col = jax.random.randint(key_col, place_shape, 0, MSIDE)
    off_row = jax.random.randint(key_drow, offset_shape, -spread, spread + 1)
    off_col = jax.random.randint(key_dcol, offset_shape, -spread, spread + 1)
    ext_row = MSIDE + place_row + off_row
    ext_col = MSIDE + place_col + off_col
    flat = (ext_row * (3 * MSIDE) + ext_col).reshape(-1)
    lowest = (MSIDE - spread) * (3 * MSIDE + 1)
    highest = (2 * MSIDE - 1 + spread) * (3 * MSIDE + 1)
    flat = flat.at[0].set(lowest).at[-1].set(highest)
    return flat.reshape(offset_shape).astype(jnp.int32)


def draw_encode_source(key, part):
    key = jax.random.fold_in(key, 1)
    extra = jax.random.randint(key, (N_PATCH, SECTORS, ENC_CAP), 0, GRID_DEV)
    slot_ids = jnp.arange(ENC_CAP)[None, None, :]
    return jnp.where(slot_ids < GRID_DEV, slot_ids, extra).astype(jnp.int32)


def draw_encode_target(key, part):
    key = jax.random.fold_in(key, 2)
    shape = (N_PATCH, SECTORS, ENC_CAP)
    return near_spot(key, shape, shape, REACH)


def draw_encode_count(key, part):
    key = jax.random.fold_in(key, 3)
    key_base, key_hot = jax.random.split(key)
    total = N_PATCH * SECTORS
    counts = jax.random.randint(key_base, (total,), GRID_DEV, ENC_CAP + 1)
    hot_device = jax.random.randint(key_hot, (), 0, total)
    cold_device = (hot_device + 1) % total
    device_ids = jnp.arange(total)
    counts = jnp.where(device_ids == hot_device, ENC_CAP, jnp.where(device_ids == cold_device, GRID_DEV, counts))
    return counts.reshape(N_PATCH, SECTORS).astype(jnp.int32)


def draw_mesh_sender(key, part):
    key = jax.random.fold_in(key, 4)
    key_pick, key_row, key_col = jax.random.split(key, 3)
    shape = (N_PATCH, SECTORS, EDGE_DEV)
    picked = jax.random.randint(key_pick, shape, 0, 16)
    offset = picked - 8
    block_id = jnp.where(picked < 8, 4, offset + (offset >= 4).astype(jnp.int32))
    block_row = block_id // 3
    block_col = block_id % 3
    inner_row = jax.random.randint(key_row, shape, 0, MSIDE)
    inner_col = jax.random.randint(key_col, shape, 0, MSIDE)
    return ((block_row * MSIDE + inner_row) * (3 * MSIDE) + block_col * MSIDE + inner_col).astype(jnp.int32)


def draw_mesh_receiver(key, part):
    key = jax.random.fold_in(key, 5)
    return jax.random.randint(key, (N_PATCH, SECTORS, EDGE_DEV), 0, MESH_DEV).astype(jnp.int32)


def draw_decode_source(key, part):
    key = jax.random.fold_in(key, 6)
    return near_spot(key, (N_PATCH, SECTORS, GRID_DEV, 1), (N_PATCH, SECTORS, GRID_DEV, DEC_DEGREE), 1)


def block_levels(key, extent, pieces, least, top_value):
    def one(dim, parts):
        steps = jax.random.uniform(jax.random.fold_in(jax.random.fold_in(key, 6), dim), (parts,), jnp.float32, least / len(pieces), top_value / len(pieces))
        return jnp.repeat(jnp.exp(steps), extent[dim] // parts).reshape((-1,) + (1,) * (len(extent) - dim - 1))

    gain = one(*pieces[0])
    for cut in pieces[1:]:
        gain = gain * one(*cut)
    return gain


def noise(own_key, extent, scale, most, cuts=(), held_as=jnp.bfloat16):
    array = jax.random.normal(own_key, extent, jnp.float32) * scale
    if len(cuts) > 0:
        array = block_levels(own_key, extent, cuts, -0.22, 0.18) * array
    return jnp.clip(array, min=-most, max=most).astype(held_as)


def setup_inputs(seed: int = 0, part: int = 0) -> dict:
    key_of = jax.random.split(jax.random.key(seed), 13)
    own_keys = jax.random.split(jax.random.fold_in(key_of[12], part), 13)
    grid_latent = noise(own_keys[0], (NGRID, D), 1.0, 6.0, ((0, 16),))
    mesh_latent = noise(own_keys[1], (NX, NY, D), 1.0, 6.0, ((0, 4), (1, 4)))
    w_first = noise(key_of[2], (5, 2 * D, D), (2 * D) ** -0.5, 0.21875, ((2, 2),))
    first_bias = noise(key_of[3], (5, D), 1.0, 4.0, (), jnp.float32)
    w_second = noise(key_of[4], (5, D, D), D ** -0.5, 0.3125, ((2, 2),))
    norm_gain = jnp.clip(1.0 + 0.1 * jax.random.normal(key_of[5], (5, D), jnp.float32), 0.5, 1.5)
    encode_source = draw_encode_source(jax.random.fold_in(key_of[12], 71), part)
    encode_target = draw_encode_target(jax.random.fold_in(key_of[12], 71), part)
    encode_count = draw_encode_count(jax.random.fold_in(key_of[12], 71), part)
    mesh_sender = draw_mesh_sender(jax.random.fold_in(key_of[12], 71), part)
    mesh_receiver = draw_mesh_receiver(jax.random.fold_in(key_of[12], 71), part)
    decode_source = draw_decode_source(jax.random.fold_in(key_of[12], 71), part)
    return dict(grid_latent=grid_latent, mesh_latent=mesh_latent, w_first=w_first, first_bias=first_bias, w_second=w_second, norm_gain=norm_gain, encode_source=encode_source, encode_target=encode_target, encode_count=encode_count, mesh_sender=mesh_sender, mesh_receiver=mesh_receiver, decode_source=decode_source)


epsilon = 1e-05

def project(rows, weight):
    return jnp.dot(rows, weight, preferred_element_type=jnp.float32)

def finish(summed, bias_layer, w_out, gain_layer):
    hidden = jax.nn.silu(summed + bias_layer).astype(jnp.bfloat16)
    result = jnp.dot(hidden, w_out, preferred_element_type=jnp.float32)
    centre = lax.optimization_barrier(jnp.mean(result, axis=-1, keepdims=True))
    shifted = result - centre
    variance = lax.optimization_barrier(jnp.mean(shifted * shifted, axis=-1, keepdims=True))
    return shifted * lax.rsqrt(variance + epsilon) * gain_layer

def to_device_major(mesh_array):
    blocks = mesh_array.reshape(N_PATCH, MSIDE, SECTORS, MSIDE, D)
    return blocks.transpose(0, 2, 1, 3, 4).reshape(-1, D)

def from_device_major(flat_mesh):
    blocks = flat_mesh.reshape(N_PATCH, SECTORS, MSIDE, MSIDE, D)
    return blocks.transpose(0, 2, 1, 3, 4).reshape(MSIDE * N_PATCH, MSIDE * SECTORS, D)

def extended_node(patch_index, ext_ids, sector_ids):
    ext_side = 3 * MSIDE
    row_global = (patch_index * MSIDE + ext_ids // ext_side - MSIDE) % NX
    col_global = (sector_ids * MSIDE + ext_ids % ext_side - MSIDE) % NY
    return ((row_global // MSIDE * SECTORS + col_global // MSIDE) * (MSIDE * MSIDE) + row_global % MSIDE * MSIDE + col_global % MSIDE).astype(jnp.int32)

def reference(grid_latent, mesh_latent, w_first, first_bias, w_second, norm_gain, encode_source, encode_target, encode_count, mesh_sender, mesh_receiver, decode_source):

    def layer_of(layer_index):
        return (first_bias[layer_index], w_second[layer_index], norm_gain[layer_index])
    mesh_block = MSIDE * MSIDE
    mesh_flat = to_device_major(mesh_latent)
    mesh_total = mesh_flat.shape[0]
    sector_col = jnp.arange(SECTORS, dtype=jnp.int32)[:, None]
    sector_cube = jnp.arange(SECTORS, dtype=jnp.int32)[:, None, None]
    slot_ids = jnp.arange(ENC_CAP, dtype=jnp.int32)[None, :]
    row_ids = jnp.arange(GRID_DEV, dtype=jnp.int32)[None, :]
    grid_send = project(grid_latent, w_first[0][:D])
    mesh_recv = project(mesh_flat, w_first[0][D:])

    def encode_patch(patch_index, total):
        sources = ((patch_index * SECTORS + sector_col) * GRID_DEV + encode_source[patch_index]).reshape(-1).astype(jnp.int32)
        targets = extended_node(patch_index, encode_target[patch_index], sector_col).reshape(-1)
        valid_slot = (slot_ids < encode_count[patch_index][:, None]).reshape(-1)
        messages = finish(grid_send[sources] + mesh_recv[targets], *layer_of(0)).astype(jnp.bfloat16)
        messages = lax.optimization_barrier(messages)
        kept = jnp.where(valid_slot[:, None], messages.astype(jnp.float32), jnp.float32(0.0))
        return total.at[targets].add(kept)
    encode_sum = lax.fori_loop(jnp.int32(0), jnp.int32(N_PATCH), encode_patch, jnp.zeros((mesh_total, D), jnp.float32))
    encode_low = encode_sum.astype(jnp.bfloat16)
    mesh_one = (mesh_flat.astype(jnp.float32) + finish(project(mesh_flat, w_first[1][:D]) + project(encode_low, w_first[1][D:]), *layer_of(1))).astype(jnp.bfloat16)
    mesh_send = project(mesh_one, w_first[2][:D])
    mesh_take = project(mesh_one, w_first[2][D:])

    def mesh_patch(patch_index, total):
        senders = extended_node(patch_index, mesh_sender[patch_index], sector_col).reshape(-1)
        receivers = ((patch_index * SECTORS + sector_col) * mesh_block + mesh_receiver[patch_index]).reshape(-1).astype(jnp.int32)
        messages = finish(mesh_send[senders] + mesh_take[receivers], *layer_of(2)).astype(jnp.bfloat16)
        messages = lax.optimization_barrier(messages)
        return total.at[receivers].add(messages.astype(jnp.float32))
    mesh_sum = lax.fori_loop(jnp.int32(0), jnp.int32(N_PATCH), mesh_patch, jnp.zeros((mesh_total, D), jnp.float32))
    mesh_low = mesh_sum.astype(jnp.bfloat16)
    mesh_two = (mesh_one.astype(jnp.float32) + finish(project(mesh_one, w_first[3][:D]) + project(mesh_low, w_first[3][D:]), *layer_of(3))).astype(jnp.bfloat16)
    mesh_give = project(mesh_two, w_first[4][:D])
    grid_take = project(grid_latent, w_first[4][D:])

    def decode_patch(patch_index):
        sources = extended_node(patch_index, decode_source[patch_index], sector_cube)
        receivers = ((patch_index * SECTORS + sector_col) * GRID_DEV + row_ids).astype(jnp.int32)
        summed = mesh_give[sources] + grid_take[receivers][:, :, None, :]
        messages = finish(summed.reshape(-1, D), *layer_of(4)).astype(jnp.bfloat16)
        messages = lax.optimization_barrier(messages)
        return lax.optimization_barrier(jnp.sum(messages.astype(jnp.float32).reshape(-1, DEC_DEGREE, D), axis=1))
    decode_sum = lax.map(decode_patch, jnp.arange(N_PATCH, dtype=jnp.int32)).reshape(-1, D)
    grid_out = (grid_latent.astype(jnp.float32) + decode_sum).astype(jnp.bfloat16)
    return (grid_out, from_device_major(mesh_two))
```

```python
import functools

import jax
import jax.numpy as jnp
import numpy as np
from jax import lax
from jax.experimental import pallas as pl
from jax.experimental.pallas import tpu as pltpu
from jax.sharding import PartitionSpec as P

EPSILON = 1e-05
MESH = pl.DeviceIdType.MESH
BF16 = jnp.bfloat16
F32 = jnp.float32
ENC_REACH = 4
DEC_REACH = 1
DIRS = ((1, 0), (-1, 0), (0, 1), (0, -1), (1, 1), (1, -1), (-1, 1), (-1, -1))


def span(step, side, reach):
    if step == 0:
        return list(range(side))
    return list(range(side - reach, side)) if step > 0 else list(range(reach))


def packing(side, reach):
    nodes, starts, sizes = [], [], []
    for dp, dc in DIRS:
        part = [i * side + j for i in span(dp, side, reach) for j in span(dc, side, reach)]
        part = part + [-1] * (-len(part) % 16)
        starts.append(len(nodes))
        sizes.append(len(part))
        nodes.extend(part)
    matrix = np.zeros((len(nodes), side * side), np.float32)
    for place, node in enumerate(nodes):
        if node >= 0:
            matrix[place, node] = 1.0
    return matrix, starts, sizes


def region_index(ext_ids, side, reach, starts):
    ext_side = 3 * side
    own = side * side
    row = (ext_ids * ((1 << 20) // ext_side + 1)) >> 20
    col = ext_ids - ext_side * row
    up, down = row < side, row >= 2 * side
    left, right = col < side, col >= 2 * side
    row_in = row - jnp.where(up, side - reach, jnp.where(down, 2 * side, side))
    col_in = col - jnp.where(left, side - reach, jnp.where(right, 2 * side, side))
    stride = jnp.where(left | right, reach, side)

    def base(dp):
        mid = own + starts[DIRS.index((dp, 0))] if dp else 0
        return jnp.where(
            left,
            own + starts[DIRS.index((dp, 1))],
            jnp.where(right, own + starts[DIRS.index((dp, -1))], mid),
        )

    offset = jnp.where(up, base(1), jnp.where(down, base(-1), base(0)))
    return offset + row_in * stride + col_in


def dot(a, b):
    return jnp.dot(a, b, preferred_element_type=F32)


def ones_where(mask):
    return jnp.where(mask, 1.0, 0.0).astype(BF16)


def columns_of(index_row):
    return jnp.transpose(jnp.broadcast_to(index_row, (128, index_row.shape[1])))


def onehot_columns(index_cols, width):
    pieces = []
    for begin in range(0, width, 128):
        size = min(128, width - begin)
        ids = lax.broadcasted_iota(jnp.int32, (index_cols.shape[0], size), 1) + begin
        pieces.append(ones_where(index_cols[:, :size] == ids))
    return pieces[0] if len(pieces) == 1 else jnp.concatenate(pieces, axis=1)


def kernel(
    sizes,
    grid_ref,
    block_ref,
    w_first_ref,
    bias_ref,
    w_second_ref,
    gain_ref,
    enc_source_ref,
    enc_target_ref,
    enc_count_ref,
    sender_ref,
    receiver_ref,
    dec_source_ref,
    enc_pack_ref,
    enc_unpack_ref,
    dec_pack_ref,
    grid_out_ref,
    mesh_out_ref,
    half_first,
    half_second,
    full_first,
    full_second,
    enc_send,
    enc_table,
    sum_send,
    sum_recv,
    mid_table,
    dec_send,
    dec_table,
    local_sem,
    weight_send_sem,
    weight_recv_sem,
    halo_send_sem,
    halo_recv_sem,
):
    n_patch, n_band, n_width = sizes
    n_cols = n_band * n_width
    group, patch = lax.axis_index("groups"), lax.axis_index("patch")
    band, core = lax.axis_index("band"), lax.axis_index("width")
    column = band * n_width + core
    n_layers, _, feat = full_first.shape
    own = block_ref.shape[0]
    side = int(round(own**0.5))
    _, enc_starts, enc_sizes = packing(side, ENC_REACH)
    _, dec_starts, dec_sizes = packing(side, DEC_REACH)
    mid_starts = [own * i for i in range(8)]

    def neighbour(dp, dc):
        there = lax.rem(column + dc + n_cols, n_cols)
        return (
            group,
            lax.rem(patch + dp + n_patch, n_patch),
            there // n_width,
            lax.rem(there, n_width),
        )

    partner = (group, patch, band, 1 - core)

    barrier = pltpu.get_barrier_semaphore()
    for dp, dc in DIRS:
        pl.semaphore_signal(barrier, inc=1, device_id=neighbour(dp, dc), device_id_type=MESH)

    local = []
    for k in range(n_layers):
        pair = []
        for s, (src, dst) in enumerate(((w_first_ref, half_first), (w_second_ref, half_second))):
            copy = pltpu.make_async_copy(src.at[k], dst.at[core, k], local_sem.at[s, k])
            copy.start()
            pair.append(copy)
        local.append(pair)

    block = block_ref[...]
    enc_send[...] = dot(enc_pack_ref[...], block).astype(BF16)
    enc_table[:own] = block
    pl.semaphore_wait(barrier, len(DIRS))

    def exchange(phase, source_of, target_of, towards=1):
        copies = []
        for d, (dp, dc) in enumerate(DIRS):
            copy = pltpu.make_async_remote_copy(
                src_ref=source_of(d),
                dst_ref=target_of(d),
                send_sem=halo_send_sem.at[phase, d],
                recv_sem=halo_recv_sem.at[phase, d],
                device_id=neighbour(towards * dp, towards * dc),
                device_id_type=MESH,
            )
            copy.start()
            copies.append(copy)
        return copies

    halo_copies = exchange(
        0,
        lambda d: enc_send.at[pl.ds(enc_starts[d], enc_sizes[d])],
        lambda d: enc_table.at[pl.ds(own + enc_starts[d], enc_sizes[d])],
    )
    remote = []
    for k in range(n_layers):
        pair = []
        for s, (src, dst) in enumerate(((w_first_ref, half_first), (w_second_ref, half_second))):
            copy = pltpu.make_async_remote_copy(
                src_ref=src.at[k],
                dst_ref=dst.at[core, k],
                send_sem=weight_send_sem.at[s, k],
                recv_sem=weight_recv_sem.at[s, k],
                device_id=partner,
                device_id_type=MESH,
            )
            copy.start()
            pair.append(copy)
        remote.append(pair)

    def take_weights(k):
        for s, (half, full) in enumerate(((half_first, full_first), (half_second, full_second))):
            local[k][s].wait()
            remote[k][s].wait_recv()
            full[k] = jnp.concatenate([half[0, k], half[1, k]], axis=-1)

    def upper(k):
        return full_first[k, :feat]

    def lower(k):
        return full_first[k, feat:]

    def finish(k, summed):
        half = 0.5 * summed
        hidden = (half + half * jnp.tanh(half)).astype(BF16)
        result = dot(hidden, full_second[k])
        centre = jnp.mean(result, axis=-1, keepdims=True)
        shifted = result - centre
        variance = jnp.mean(shifted * shifted, axis=-1, keepdims=True)
        return shifted * lax.rsqrt(variance + EPSILON) * gain_ref[k : k + 1, :]

    def bias(k):
        return bias_ref[k : k + 1, :]

    grid = grid_ref[...]
    n_grid = grid.shape[0]
    n_enc = enc_target_ref.shape[1]
    own_enc = min(n_grid, n_enc)
    source_cols = columns_of(enc_source_ref[...][:, own_enc:])
    more = dot(onehot_columns(source_cols, n_grid), grid).astype(BF16)
    sending = jnp.concatenate([grid, more], axis=0)
    n_enc_rows = own + sum(enc_sizes)
    target_row = region_index(enc_target_ref[...], side, ENC_REACH, enc_starts)
    target_onehot = onehot_columns(columns_of(target_row), n_enc_rows)
    slot_ids = lax.broadcasted_iota(jnp.int32, (1, n_enc), 1)
    kept_row = jnp.where(slot_ids < enc_count_ref[...], target_row, -1)
    node_ids = lax.broadcasted_iota(jnp.int32, (n_enc_rows, n_enc), 0)
    scatter = ones_where(node_ids == kept_row)
    take_weights(0)
    grid_term = dot(sending, upper(0)) + bias(0)
    for copy in halo_copies:
        copy.wait_recv()
    target_rows = dot(target_onehot, enc_table[...]).astype(BF16)
    messages = finish(0, grid_term + dot(target_rows, lower(0))).astype(BF16)
    partial = dot(scatter, messages)
    sum_send[...] = partial[own:].astype(BF16)
    sum_copies = exchange(
        1,
        lambda d: sum_send.at[pl.ds(enc_starts[d], enc_sizes[d])],
        lambda d: sum_recv.at[pl.ds(enc_starts[d], enc_sizes[d])],
        -1,
    )

    take_weights(1)
    node_term = dot(block, upper(1)) + bias(1)
    take_weights(2)
    take_weights(3)
    for copy in sum_copies:
        copy.wait_recv()
    encode_sum = partial[:own] + dot(enc_unpack_ref[...], sum_recv[...])
    node_pre = node_term + dot(encode_sum.astype(BF16), lower(1))
    mesh_one = (block.astype(F32) + finish(1, node_pre)).astype(BF16)
    mid_table[0] = mesh_one
    mid_copies = exchange(2, lambda d: mid_table.at[0], lambda d: mid_table.at[1 + d])

    receiver_row = receiver_ref[...]
    n_edges = receiver_row.shape[1]
    taking_rows = dot(onehot_columns(columns_of(receiver_row), own), mesh_one).astype(BF16)
    edge_term = dot(taking_rows, lower(2)) + bias(2)
    own_ids = lax.broadcasted_iota(jnp.int32, (own, n_edges), 0)
    edge_scatter = ones_where(own_ids == receiver_row)
    sender_row = region_index(sender_ref[...], side, side, mid_starts)
    sender_onehot = onehot_columns(columns_of(sender_row), 9 * own)
    node_term_two = dot(mesh_one, upper(3)) + bias(3)
    take_weights(4)
    grid_taking = dot(grid, lower(4)) + bias(4)
    n_dec_rows = own + sum(dec_sizes)
    for copy in mid_copies:
        copy.wait_recv()
    sending_rows = dot(sender_onehot, mid_table[...].reshape(9 * own, feat)).astype(BF16)
    edge_messages = finish(2, edge_term + dot(sending_rows, upper(2))).astype(BF16)
    mesh_sum = dot(edge_scatter, edge_messages)
    node_pre_two = node_term_two + dot(mesh_sum.astype(BF16), lower(3))
    mesh_two = (mesh_one.astype(F32) + finish(3, node_pre_two)).astype(BF16)
    mesh_out_ref[...] = mesh_two
    dec_send[...] = dot(dec_pack_ref[...], mesh_two).astype(BF16)
    dec_table[:own] = mesh_two
    dec_copies = exchange(
        3,
        lambda d: dec_send.at[pl.ds(dec_starts[d], dec_sizes[d])],
        lambda d: dec_table.at[pl.ds(own + dec_starts[d], dec_sizes[d])],
    )

    dec_rows = region_index(dec_source_ref[...], side, DEC_REACH, dec_starts)
    dec_ids = lax.broadcasted_iota(jnp.int32, (n_grid, n_dec_rows), 1)
    dec_onehots = [
        ones_where(dec_rows[:, k : k + 1] == dec_ids) for k in range(dec_rows.shape[1])
    ]
    for copy in dec_copies:
        copy.wait_recv()
    table = dec_table[...]
    total = grid.astype(F32)
    decode_sum = None
    for onehot in dec_onehots:
        giving_rows = dot(onehot, table).astype(BF16)
        message = finish(4, grid_taking + dot(giving_rows, upper(4))).astype(BF16).astype(F32)
        decode_sum = message if decode_sum is None else decode_sum + message
    grid_out_ref[...] = (total + decode_sum).astype(BF16)

    for copies in remote + [halo_copies, sum_copies, mid_copies, dec_copies]:
        for copy in copies:
            copy.wait_send()


def per_device(
    sizes,
    grid_latent,
    mesh_latent,
    w_first,
    first_bias,
    w_second,
    norm_gain,
    encode_source,
    encode_target,
    encode_count,
    mesh_sender,
    mesh_receiver,
    decode_source,
):
    side, _, feat = mesh_latent.shape
    own = side * side
    n_layers = w_first.shape[0]
    share = w_first.shape[2]
    enc_matrix, _, enc_sizes = packing(side, ENC_REACH)
    dec_matrix, _, dec_sizes = packing(side, DEC_REACH)
    n_enc, n_dec = sum(enc_sizes), sum(dec_sizes)
    vmem = pl.BlockSpec(memory_space=pltpu.VMEM)
    anywhere = pl.BlockSpec(memory_space=pl.ANY)
    grid_out, mesh_out = pl.pallas_call(
        functools.partial(kernel, sizes),
        out_shape=(
            jax.ShapeDtypeStruct(grid_latent.shape, BF16),
            jax.ShapeDtypeStruct((own, feat), BF16),
        ),
        in_specs=[vmem, vmem, anywhere, vmem, anywhere] + [vmem] * 10,
        out_specs=(vmem, vmem),
        scratch_shapes=[
            pltpu.VMEM((2, n_layers, 2 * feat, share), BF16),
            pltpu.VMEM((2, n_layers, feat, share), BF16),
            pltpu.VMEM((n_layers, 2 * feat, feat), BF16),
            pltpu.VMEM((n_layers, feat, feat), BF16),
            pltpu.VMEM((n_enc, feat), BF16),
            pltpu.VMEM((own + n_enc, feat), BF16),
            pltpu.VMEM((n_enc, feat), BF16),
            pltpu.VMEM((n_enc, feat), BF16),
            pltpu.VMEM((9, own, feat), BF16),
            pltpu.VMEM((n_dec, feat), BF16),
            pltpu.VMEM((own + n_dec, feat), BF16),
            pltpu.SemaphoreType.DMA((2, n_layers)),
            pltpu.SemaphoreType.DMA((2, n_layers)),
            pltpu.SemaphoreType.DMA((2, n_layers)),
            pltpu.SemaphoreType.DMA((4, 8)),
            pltpu.SemaphoreType.DMA((4, 8)),
        ],
        compiler_params=pltpu.CompilerParams(
            collective_id=0, has_side_effects=True, vmem_limit_bytes=48 * 1024 * 1024
        ),
    )(
        grid_latent,
        mesh_latent.reshape(own, feat),
        w_first,
        first_bias,
        w_second,
        norm_gain,
        encode_source.reshape(1, -1),
        encode_target.reshape(1, -1),
        encode_count.reshape(1, 1),
        mesh_sender.reshape(1, -1),
        mesh_receiver.reshape(1, -1),
        decode_source.reshape(decode_source.shape[2:]),
        jnp.asarray(enc_matrix, BF16),
        jnp.asarray(enc_matrix.T, BF16),
        jnp.asarray(dec_matrix, BF16),
    )
    return grid_out, mesh_out.reshape(mesh_latent.shape)


def solution(mesh):
    sizes = tuple(mesh.shape[name] for name in ("patch", "band", "width"))
    in_specs = (
        P(("groups", "patch", "band", "width"), None),
        P(("groups", "patch"), ("band", "width"), None),
        P(None, None, "width"),
        P(),
        P(None, None, "width"),
        P(),
        P("patch", ("band", "width"), None),
        P("patch", ("band", "width"), None),
        P("patch", ("band", "width")),
        P("patch", ("band", "width"), None),
        P("patch", ("band", "width"), None),
        P("patch", ("band", "width"), None, None),
    )
    out_specs = (
        P(("groups", "patch", "band", "width"), None),
        P(("groups", "patch"), ("band", "width"), None),
    )
    return jax.shard_map(
        functools.partial(per_device, sizes),
        mesh=mesh,
        in_specs=in_specs,
        out_specs=out_specs,
        check_vma=False,
    )
```

```python
import functools

import jax
import jax.numpy as jnp
import numpy as np
from jax import lax
from jax.experimental import pallas as pl
from jax.experimental.pallas import tpu as pltpu
from jax.sharding import PartitionSpec as P

EPSILON = 1e-05
MESH = pl.DeviceIdType.MESH
BF16 = jnp.bfloat16
F32 = jnp.float32
ENC_REACH = 4
DEC_REACH = 1
DIRS = ((1, 0), (-1, 0), (0, 1), (0, -1), (1, 1), (1, -1), (-1, 1), (-1, -1))


def span(step, side, reach):
    if step == 0:
        return list(range(side))
    return list(range(side - reach, side)) if step > 0 else list(range(reach))


def packing(side, reach):
    nodes, starts, sizes = [], [], []
    for dp, dc in DIRS:
        part = [i * side + j for i in span(dp, side, reach) for j in span(dc, side, reach)]
        part = part + [-1] * (-len(part) % 16)
        starts.append(len(nodes))
        sizes.append(len(part))
        nodes.extend(part)
    matrix = np.zeros((len(nodes), side * side), np.float32)
    for place, node in enumerate(nodes):
        if node >= 0:
            matrix[place, node] = 1.0
    return matrix, starts, sizes


def region_index(ext_ids, side, reach, starts):
    ext_side = 3 * side
    own = side * side
    row = (ext_ids * ((1 << 20) // ext_side + 1)) >> 20
    col = ext_ids - ext_side * row
    up, down = row < side, row >= 2 * side
    left, right = col < side, col >= 2 * side
    row_in = row - jnp.where(up, side - reach, jnp.where(down, 2 * side, side))
    col_in = col - jnp.where(left, side - reach, jnp.where(right, 2 * side, side))
    stride = jnp.where(left | right, reach, side)

    def base(dp):
        mid = own + starts[DIRS.index((dp, 0))] if dp else 0
        return jnp.where(
            left,
            own + starts[DIRS.index((dp, 1))],
            jnp.where(right, own + starts[DIRS.index((dp, -1))], mid),
        )

    offset = jnp.where(up, base(1), jnp.where(down, base(-1), base(0)))
    return offset + row_in * stride + col_in


def dot(a, b):
    return jnp.dot(a, b, preferred_element_type=F32)


def dot_t(a, b):
    return lax.dot_general(a, b, (((1,), (1,)), ((), ())), preferred_element_type=F32)


def ones_where(mask):
    return jnp.where(mask, 1.0, 0.0).astype(BF16)


def columns_of(index_row):
    return jnp.transpose(jnp.broadcast_to(index_row, (128, index_row.shape[1])))


def onehot_columns(index_cols, width):
    pieces = []
    for begin in range(0, width, 128):
        size = min(128, width - begin)
        ids = lax.broadcasted_iota(jnp.int32, (index_cols.shape[0], size), 1) + begin
        pieces.append(ones_where(index_cols[:, :size] == ids))
    return pieces[0] if len(pieces) == 1 else jnp.concatenate(pieces, axis=1)


STAGED = 13


def kernel(sizes, *refs):
    w_first_ref, w_second_ref = refs[:2]
    staged_hbm = refs[2 : 2 + STAGED]
    grid_out_ref, mesh_out_ref = refs[2 + STAGED : 4 + STAGED]
    staged = refs[4 + STAGED : 4 + 2 * STAGED]
    (
        grid_ref,
        block_ref,
        bias_ref,
        gain_ref,
        enc_source_ref,
        enc_target_ref,
        enc_count_ref,
        sender_ref,
        receiver_ref,
        dec_source_ref,
        enc_pack_ref,
        enc_unpack_ref,
        dec_pack_ref,
    ) = staged
    (
        full_first,
        full_second,
        enc_send,
        enc_table,
        sum_send,
        sum_recv,
        mid_table,
        dec_send,
        dec_table,
        staged_sem,
        local_sem,
        weight_send_sem,
        weight_recv_sem,
        halo_send_sem,
        halo_recv_sem,
    ) = refs[4 + 2 * STAGED :]
    n_patch, n_band, n_width = sizes
    n_cols = n_band * n_width
    group, patch = lax.axis_index("groups"), lax.axis_index("patch")
    band, core = lax.axis_index("band"), lax.axis_index("width")
    column = band * n_width + core
    n_layers, feat, _ = full_first.shape
    share = w_first_ref.shape[1]
    own_rows = pl.ds(pl.multiple_of(core * share, 16), share)
    own = block_ref.shape[0]
    side = int(round(own**0.5))
    _, enc_starts, enc_sizes = packing(side, ENC_REACH)
    _, dec_starts, dec_sizes = packing(side, DEC_REACH)
    mid_starts = [own * i for i in range(8)]

    def neighbour(dp, dc):
        there = lax.rem(column + dc + n_cols, n_cols)
        return (
            group,
            lax.rem(patch + dp + n_patch, n_patch),
            there // n_width,
            lax.rem(there, n_width),
        )

    partner = (group, patch, band, 1 - core)

    barrier = pltpu.get_barrier_semaphore()
    for dp, dc in DIRS:
        pl.semaphore_signal(barrier, inc=1, device_id=neighbour(dp, dc), device_id_type=MESH)

    staging = []
    for i in range(STAGED):
        copy = pltpu.make_async_copy(staged_hbm[i], staged[i], staged_sem.at[i])
        copy.start()
        staging.append(copy)
    local = []
    for k in range(n_layers):
        pair = []
        for s, (src, dst) in enumerate(((w_first_ref, full_first), (w_second_ref, full_second))):
            copy = pltpu.make_async_copy(src.at[k], dst.at[k, own_rows], local_sem.at[s, k])
            copy.start()
            pair.append(copy)
        local.append(pair)

    for copy in staging:
        copy.wait()
    block = block_ref[...]
    enc_send[...] = dot(enc_pack_ref[...], block).astype(BF16)
    enc_table[:own] = block
    pl.semaphore_wait(barrier, len(DIRS))

    def exchange(phase, source_of, target_of, towards=1, chosen=None):
        copies = []
        for d in range(len(DIRS)) if chosen is None else chosen:
            dp, dc = DIRS[d][0], DIRS[d][1]
            if chosen and len(chosen) < 4:
                dp = 0
            copy = pltpu.make_async_remote_copy(
                src_ref=source_of(d),
                dst_ref=target_of(d),
                send_sem=halo_send_sem.at[phase, d],
                recv_sem=halo_recv_sem.at[phase, d],
                device_id=neighbour(towards * dp, towards * dc),
                device_id_type=MESH,
            )
            copy.start()
            copies.append(copy)
        return copies

    halo_copies = exchange(
        0,
        lambda d: enc_send.at[pl.ds(enc_starts[d], enc_sizes[d])],
        lambda d: enc_table.at[pl.ds(own + enc_starts[d], enc_sizes[d])],
    )
    remote = []
    for k in range(n_layers):
        pair = []
        for s, (src, dst) in enumerate(((w_first_ref, full_first), (w_second_ref, full_second))):
            copy = pltpu.make_async_remote_copy(
                src_ref=src.at[k],
                dst_ref=dst.at[k, own_rows],
                send_sem=weight_send_sem.at[s, k],
                recv_sem=weight_recv_sem.at[s, k],
                device_id=partner,
                device_id_type=MESH,
            )
            copy.start()
            pair.append(copy)
        remote.append(pair)

    def take_weights(k):
        for s in range(2):
            local[k][s].wait()
            remote[k][s].wait_recv()

    def upper(k):
        return full_first[k, :, :feat]

    def lower(k):
        return full_first[k, :, feat:]

    def finish(k, summed):
        half = 0.5 * summed
        hidden = (half + half * jnp.tanh(half)).astype(BF16)
        result = dot_t(hidden, full_second[k])
        centre = jnp.mean(result, axis=-1, keepdims=True)
        shifted = result - centre
        variance = jnp.mean(shifted * shifted, axis=-1, keepdims=True)
        return shifted * lax.rsqrt(variance + EPSILON) * gain_ref[k : k + 1, :]

    def bias(k):
        return bias_ref[k : k + 1, :]

    grid = grid_ref[...]
    n_grid = grid.shape[0]
    n_enc = enc_target_ref.shape[1]
    own_enc = min(n_grid, n_enc)
    source_cols = columns_of(enc_source_ref[...][:, own_enc:])
    more = dot(onehot_columns(source_cols, n_grid), grid).astype(BF16)
    sending = jnp.concatenate([grid, more], axis=0)
    n_enc_rows = own + sum(enc_sizes)
    target_row = region_index(enc_target_ref[...], side, ENC_REACH, enc_starts)
    target_onehot = onehot_columns(columns_of(target_row), n_enc_rows)
    slot_ids = lax.broadcasted_iota(jnp.int32, (1, n_enc), 1)
    kept_row = jnp.where(slot_ids < enc_count_ref[...], target_row, -1)
    node_ids = lax.broadcasted_iota(jnp.int32, (n_enc_rows, n_enc), 0)
    scatter = ones_where(node_ids == kept_row)
    take_weights(0)
    grid_term = dot_t(sending, upper(0)) + bias(0)
    for copy in halo_copies:
        copy.wait_recv()
    target_rows = dot(target_onehot, enc_table[...]).astype(BF16)
    messages = finish(0, grid_term + dot_t(target_rows, lower(0))).astype(BF16)
    partial = dot(scatter, messages)
    sum_send[...] = partial[own:].astype(BF16)
    sum_copies = exchange(
        1,
        lambda d: sum_send.at[pl.ds(enc_starts[d], enc_sizes[d])],
        lambda d: sum_recv.at[pl.ds(enc_starts[d], enc_sizes[d])],
        -1,
    )

    take_weights(1)
    node_term = dot_t(block, upper(1)) + bias(1)
    take_weights(2)
    take_weights(3)
    for copy in sum_copies:
        copy.wait_recv()
    encode_sum = partial[:own] + dot(enc_unpack_ref[...], sum_recv[...])
    node_pre = node_term + dot_t(encode_sum.astype(BF16), lower(1))
    mesh_one = (block.astype(F32) + finish(1, node_pre)).astype(BF16)
    mid_table[0] = mesh_one
    mid_copies = exchange(
        2, lambda d: mid_table.at[0], lambda d: mid_table.at[1 + d], 1, (0, 1, 2, 3)
    )

    receiver_row = receiver_ref[...]
    n_edges = receiver_row.shape[1]
    taking_rows = dot(onehot_columns(columns_of(receiver_row), own), mesh_one).astype(BF16)
    edge_term = dot_t(taking_rows, lower(2)) + bias(2)
    for d in range(2):
        mid_copies[d].wait_recv()
        corners = (4 + 2 * d, 5 + 2 * d)
        mid_copies = mid_copies + exchange(
            2, lambda c: mid_table.at[1 + d], lambda c: mid_table.at[1 + c], 1, corners
        )
    own_ids = lax.broadcasted_iota(jnp.int32, (own, n_edges), 0)
    edge_scatter = ones_where(own_ids == receiver_row)
    sender_row = region_index(sender_ref[...], side, side, mid_starts)
    sender_onehot = onehot_columns(columns_of(sender_row), 9 * own)
    node_term_two = dot_t(mesh_one, upper(3)) + bias(3)
    take_weights(4)
    grid_taking = dot_t(grid, lower(4)) + bias(4)
    n_dec_rows = own + sum(dec_sizes)
    for copy in mid_copies[2:]:
        copy.wait_recv()
    sending_rows = dot(sender_onehot, mid_table[...].reshape(9 * own, feat)).astype(BF16)
    edge_messages = finish(2, edge_term + dot_t(sending_rows, upper(2))).astype(BF16)
    mesh_sum = dot(edge_scatter, edge_messages)
    node_pre_two = node_term_two + dot_t(mesh_sum.astype(BF16), lower(3))
    mesh_two = (mesh_one.astype(F32) + finish(3, node_pre_two)).astype(BF16)
    mesh_out_ref[...] = mesh_two
    dec_send[...] = dot(dec_pack_ref[...], mesh_two).astype(BF16)
    dec_table[:own] = mesh_two
    dec_copies = exchange(
        3,
        lambda d: dec_send.at[pl.ds(dec_starts[d], dec_sizes[d])],
        lambda d: dec_table.at[pl.ds(own + dec_starts[d], dec_sizes[d])],
    )

    dec_onehots = [
        onehot_columns(
            columns_of(region_index(dec_source_ref[k], side, DEC_REACH, dec_starts)), n_dec_rows
        )
        for k in range(dec_source_ref.shape[0])
    ]
    for copy in dec_copies:
        copy.wait_recv()
    table = dec_table[...]
    total = grid.astype(F32)
    decode_sum = None
    for onehot in dec_onehots:
        giving_rows = dot(onehot, table).astype(BF16)
        message = finish(4, grid_taking + dot_t(giving_rows, upper(4))).astype(BF16).astype(F32)
        decode_sum = message if decode_sum is None else decode_sum + message
    grid_out_ref[...] = (total + decode_sum).astype(BF16)

    for copies in remote + [halo_copies, sum_copies, mid_copies, dec_copies]:
        for copy in copies:
            copy.wait_send()


def per_device(
    sizes,
    grid_latent,
    mesh_latent,
    w_first,
    first_bias,
    w_second,
    norm_gain,
    encode_source,
    encode_target,
    encode_count,
    mesh_sender,
    mesh_receiver,
    decode_source,
):
    side, _, feat = mesh_latent.shape
    own = side * side
    n_layers = w_first.shape[0]
    enc_matrix, _, enc_sizes = packing(side, ENC_REACH)
    dec_matrix, _, dec_sizes = packing(side, DEC_REACH)
    n_enc, n_dec = sum(enc_sizes), sum(dec_sizes)
    vmem = pl.BlockSpec(memory_space=pltpu.VMEM)
    anywhere = pl.BlockSpec(memory_space=pl.ANY)
    staged = (
        grid_latent,
        mesh_latent.reshape(own, feat),
        first_bias,
        norm_gain,
        encode_source.reshape(1, -1),
        encode_target.reshape(1, -1),
        encode_count.reshape(1, 1),
        mesh_sender.reshape(1, -1),
        mesh_receiver.reshape(1, -1),
        decode_source.transpose(0, 1, 3, 2).reshape(decode_source.shape[3], 1, -1),
        jnp.asarray(enc_matrix, BF16),
        jnp.asarray(enc_matrix.T, BF16),
        jnp.asarray(dec_matrix, BF16),
    )
    grid_out, mesh_out = pl.pallas_call(
        functools.partial(kernel, sizes),
        out_shape=(
            jax.ShapeDtypeStruct(grid_latent.shape, BF16),
            jax.ShapeDtypeStruct((own, feat), BF16),
        ),
        in_specs=[anywhere] * (2 + STAGED),
        out_specs=(vmem, vmem),
        scratch_shapes=[pltpu.VMEM(array.shape, array.dtype) for array in staged]
        + [
            pltpu.VMEM((n_layers, feat, 2 * feat), BF16),
            pltpu.VMEM((n_layers, feat, feat), BF16),
            pltpu.VMEM((n_enc, feat), BF16),
            pltpu.VMEM((own + n_enc, feat), BF16),
            pltpu.VMEM((n_enc, feat), BF16),
            pltpu.VMEM((n_enc, feat), BF16),
            pltpu.VMEM((9, own, feat), BF16),
            pltpu.VMEM((n_dec, feat), BF16),
            pltpu.VMEM((own + n_dec, feat), BF16),
            pltpu.SemaphoreType.DMA((STAGED,)),
            pltpu.SemaphoreType.DMA((2, n_layers)),
            pltpu.SemaphoreType.DMA((2, n_layers)),
            pltpu.SemaphoreType.DMA((2, n_layers)),
            pltpu.SemaphoreType.DMA((4, 8)),
            pltpu.SemaphoreType.DMA((4, 8)),
        ],
        compiler_params=pltpu.CompilerParams(
            collective_id=0, has_side_effects=True, vmem_limit_bytes=60 * 1024 * 1024
        ),
    )(w_first.transpose(0, 2, 1), w_second.transpose(0, 2, 1), *staged)
    return grid_out, mesh_out.reshape(mesh_latent.shape)


def solution(mesh):
    sizes = tuple(mesh.shape[name] for name in ("patch", "band", "width"))
    in_specs = (
        P(("groups", "patch", "band", "width"), None),
        P(("groups", "patch"), ("band", "width"), None),
        P(None, None, "width"),
        P(),
        P(None, None, "width"),
        P(),
        P("patch", ("band", "width"), None),
        P("patch", ("band", "width"), None),
        P("patch", ("band", "width")),
        P("patch", ("band", "width"), None),
        P("patch", ("band", "width"), None),
        P("patch", ("band", "width"), None, None),
    )
    out_specs = (
        P(("groups", "patch", "band", "width"), None),
        P(("groups", "patch"), ("band", "width"), None),
    )
    return jax.shard_map(
        functools.partial(per_device, sizes),
        mesh=mesh,
        in_specs=in_specs,
        out_specs=out_specs,
        check_vma=False,
    )
```

```python
import functools

import jax
import jax.numpy as jnp
import numpy as np
from jax import lax
from jax.experimental import pallas as pl
from jax.experimental.pallas import tpu as pltpu
from jax.sharding import PartitionSpec as P

EPSILON = 1e-05
MESH = pl.DeviceIdType.MESH
BF16 = jnp.bfloat16
F32 = jnp.float32
ENC_REACH = 4
DEC_REACH = 1
DIRS = ((1, 0), (-1, 0), (0, 1), (0, -1), (1, 1), (1, -1), (-1, 1), (-1, -1))


def span(step, side, reach):
    if step == 0:
        return list(range(side))
    return list(range(side - reach, side)) if step > 0 else list(range(reach))


def packing(side, reach):
    nodes, starts, sizes = [], [], []
    for dp, dc in DIRS:
        part = [i * side + j for i in span(dp, side, reach) for j in span(dc, side, reach)]
        part = part + [-1] * (-len(part) % 16)
        starts.append(len(nodes))
        sizes.append(len(part))
        nodes.extend(part)
    matrix = np.zeros((len(nodes), side * side), np.float32)
    for place, node in enumerate(nodes):
        if node >= 0:
            matrix[place, node] = 1.0
    return matrix, starts, sizes


def region_index(ext_ids, side, reach, starts):
    ext_side = 3 * side
    own = side * side
    row = (ext_ids * ((1 << 20) // ext_side + 1)) >> 20
    col = ext_ids - ext_side * row
    up, down = row < side, row >= 2 * side
    left, right = col < side, col >= 2 * side
    row_in = row - jnp.where(up, side - reach, jnp.where(down, 2 * side, side))
    col_in = col - jnp.where(left, side - reach, jnp.where(right, 2 * side, side))
    stride = jnp.where(left | right, reach, side)

    def base(dp):
        mid = own + starts[DIRS.index((dp, 0))] if dp else 0
        return jnp.where(
            left,
            own + starts[DIRS.index((dp, 1))],
            jnp.where(right, own + starts[DIRS.index((dp, -1))], mid),
        )

    offset = jnp.where(up, base(1), jnp.where(down, base(-1), base(0)))
    return offset + row_in * stride + col_in


def dot(a, b):
    return jnp.dot(a, b, preferred_element_type=F32)


def dot_t(a, b):
    return lax.dot_general(a, b, (((1,), (1,)), ((), ())), preferred_element_type=F32)


def ones_where(mask):
    return jnp.where(mask, 1.0, 0.0).astype(BF16)


def columns_of(index_row):
    return jnp.transpose(jnp.broadcast_to(index_row, (128, index_row.shape[1])))


def onehot_columns(index_cols, width):
    pieces = []
    for begin in range(0, width, 128):
        size = min(128, width - begin)
        ids = lax.broadcasted_iota(jnp.int32, (index_cols.shape[0], size), 1) + begin
        pieces.append(ones_where(index_cols[:, :size] == ids))
    return pieces[0] if len(pieces) == 1 else jnp.concatenate(pieces, axis=1)


STAGED = 13


def kernel(sizes, *refs):
    w_first_ref, w_second_ref = refs[:2]
    staged_hbm = refs[2 : 2 + STAGED]
    grid_out_ref, mesh_out_ref = refs[2 + STAGED : 4 + STAGED]
    staged = refs[4 + STAGED : 4 + 2 * STAGED]
    (
        grid_ref,
        block_ref,
        bias_ref,
        gain_ref,
        enc_source_ref,
        enc_target_ref,
        enc_count_ref,
        sender_ref,
        receiver_ref,
        dec_source_ref,
        enc_pack_ref,
        enc_unpack_ref,
        dec_pack_ref,
    ) = staged
    (
        full_first,
        full_second,
        enc_send,
        enc_table,
        sum_send,
        sum_recv,
        mid_table,
        dec_send,
        dec_table,
        staged_sem,
        local_sem,
        weight_send_sem,
        weight_recv_sem,
        halo_send_sem,
        halo_recv_sem,
    ) = refs[4 + 2 * STAGED :]
    n_patch, n_band, n_width = sizes
    n_cols = n_band * n_width
    group, patch = lax.axis_index("groups"), lax.axis_index("patch")
    band, core = lax.axis_index("band"), lax.axis_index("width")
    column = band * n_width + core
    n_layers, feat, _ = full_first.shape
    share = w_first_ref.shape[1]
    own_rows = pl.ds(pl.multiple_of(core * share, 16), share)
    own = block_ref.shape[0]
    side = int(round(own**0.5))
    _, enc_starts, enc_sizes = packing(side, ENC_REACH)
    _, dec_starts, dec_sizes = packing(side, DEC_REACH)
    mid_starts = [own * i for i in range(8)]

    def neighbour(dp, dc):
        there = lax.rem(column + dc + n_cols, n_cols)
        return (
            group,
            lax.rem(patch + dp + n_patch, n_patch),
            there // n_width,
            lax.rem(there, n_width),
        )

    partner = (group, patch, band, 1 - core)

    barrier = pltpu.get_barrier_semaphore()
    for dp, dc in DIRS:
        pl.semaphore_signal(barrier, inc=1, device_id=neighbour(dp, dc), device_id_type=MESH)

    staging = []
    for i in range(STAGED):
        copy = pltpu.make_async_copy(staged_hbm[i], staged[i], staged_sem.at[i])
        copy.start()
        staging.append(copy)
    local = []
    for k in range(n_layers):
        pair = []
        for s, (src, dst) in enumerate(((w_first_ref, full_first), (w_second_ref, full_second))):
            copy = pltpu.make_async_copy(src.at[k], dst.at[k, own_rows], local_sem.at[s, k])
            copy.start()
            pair.append(copy)
        local.append(pair)

    for copy in staging:
        copy.wait()
    block = block_ref[...]
    enc_send[...] = dot(enc_pack_ref[...], block).astype(BF16)
    enc_table[:own] = block
    pl.semaphore_wait(barrier, len(DIRS))

    def exchange(phase, source_of, target_of, towards=1, chosen=None):
        copies = []
        for d in (0, 1, 4, 5, 6, 7, 2, 3) if chosen is None else chosen:
            dp, dc = DIRS[d][0], DIRS[d][1]
            if chosen and len(chosen) < 4:
                dp = 0
            copy = pltpu.make_async_remote_copy(
                src_ref=source_of(d),
                dst_ref=target_of(d),
                send_sem=halo_send_sem.at[phase, d],
                recv_sem=halo_recv_sem.at[phase, d],
                device_id=neighbour(towards * dp, towards * dc),
                device_id_type=MESH,
            )
            copy.start()
            copies.append(copy)
        return copies

    halo_copies = exchange(
        0,
        lambda d: enc_send.at[pl.ds(enc_starts[d], enc_sizes[d])],
        lambda d: enc_table.at[pl.ds(own + enc_starts[d], enc_sizes[d])],
    )
    remote = []
    for k in range(n_layers):
        pair = []
        for s, (src, dst) in enumerate(((w_first_ref, full_first), (w_second_ref, full_second))):
            copy = pltpu.make_async_remote_copy(
                src_ref=src.at[k],
                dst_ref=dst.at[k, own_rows],
                send_sem=weight_send_sem.at[s, k],
                recv_sem=weight_recv_sem.at[s, k],
                device_id=partner,
                device_id_type=MESH,
            )
            copy.start()
            pair.append(copy)
        remote.append(pair)

    def take_weights(k):
        for s in range(2):
            local[k][s].wait()
            remote[k][s].wait_recv()

    def upper(k):
        return full_first[k, :, :feat]

    def lower(k):
        return full_first[k, :, feat:]

    def finish(k, summed):
        half = 0.5 * summed
        hidden = (half + half * jnp.tanh(half)).astype(BF16)
        result = dot_t(hidden, full_second[k])
        centre = jnp.mean(result, axis=-1, keepdims=True)
        shifted = result - centre
        variance = jnp.mean(shifted * shifted, axis=-1, keepdims=True)
        return shifted * lax.rsqrt(variance + EPSILON) * gain_ref[k : k + 1, :]

    def bias(k):
        return bias_ref[k : k + 1, :]

    grid = grid_ref[...]
    n_grid = grid.shape[0]
    n_enc = enc_target_ref.shape[1]
    own_enc = min(n_grid, n_enc)
    source_cols = columns_of(enc_source_ref[...][:, own_enc:])
    more = dot(onehot_columns(source_cols, n_grid), grid).astype(BF16)
    sending = jnp.concatenate([grid, more], axis=0)
    n_enc_rows = own + sum(enc_sizes)
    target_row = region_index(enc_target_ref[...], side, ENC_REACH, enc_starts)
    target_onehot = onehot_columns(columns_of(target_row), n_enc_rows)
    slot_ids = lax.broadcasted_iota(jnp.int32, (1, n_enc), 1)
    kept_row = jnp.where(slot_ids < enc_count_ref[...], target_row, -1)
    node_ids = lax.broadcasted_iota(jnp.int32, (n_enc_rows, n_enc), 0)
    scatter = ones_where(node_ids == kept_row)
    take_weights(0)
    grid_term = dot_t(sending, upper(0)) + bias(0)
    for copy in halo_copies:
        copy.wait_recv()
    target_rows = dot(target_onehot, enc_table[...]).astype(BF16)
    messages = finish(0, grid_term + dot_t(target_rows, lower(0))).astype(BF16)
    partial = dot(scatter, messages)
    sum_send[...] = partial[own:].astype(BF16)
    sum_copies = exchange(
        1,
        lambda d: sum_send.at[pl.ds(enc_starts[d], enc_sizes[d])],
        lambda d: sum_recv.at[pl.ds(enc_starts[d], enc_sizes[d])],
        -1,
    )

    take_weights(1)
    node_term = dot_t(block, upper(1)) + bias(1)
    take_weights(2)
    take_weights(3)
    for copy in sum_copies:
        copy.wait_recv()
    encode_sum = partial[:own] + dot(enc_unpack_ref[...], sum_recv[...])
    node_pre = node_term + dot_t(encode_sum.astype(BF16), lower(1))
    mesh_one = (block.astype(F32) + finish(1, node_pre)).astype(BF16)
    mid_table[0] = mesh_one
    mid_copies = exchange(
        2, lambda d: mid_table.at[0], lambda d: mid_table.at[1 + d], 1, (0, 1, 2, 3)
    )

    receiver_row = receiver_ref[...]
    n_edges = receiver_row.shape[1]
    taking_rows = dot(onehot_columns(columns_of(receiver_row), own), mesh_one).astype(BF16)
    edge_term = dot_t(taking_rows, lower(2)) + bias(2)
    for d in range(2):
        mid_copies[d].wait_recv()
        corners = (4 + 2 * d, 5 + 2 * d)
        mid_copies = mid_copies + exchange(
            2, lambda c: mid_table.at[1 + d], lambda c: mid_table.at[1 + c], 1, corners
        )
    own_ids = lax.broadcasted_iota(jnp.int32, (own, n_edges), 0)
    edge_scatter = ones_where(own_ids == receiver_row)
    sender_row = region_index(sender_ref[...], side, side, mid_starts)
    sender_onehot = onehot_columns(columns_of(sender_row), 9 * own)
    node_term_two = dot_t(mesh_one, upper(3)) + bias(3)
    take_weights(4)
    grid_taking = dot_t(grid, lower(4)) + bias(4)
    n_dec_rows = own + sum(dec_sizes)
    for copy in mid_copies[2:]:
        copy.wait_recv()
    sending_rows = dot(sender_onehot, mid_table[...].reshape(9 * own, feat)).astype(BF16)
    edge_messages = finish(2, edge_term + dot_t(sending_rows, upper(2))).astype(BF16)
    mesh_sum = dot(edge_scatter, edge_messages)
    node_pre_two = node_term_two + dot_t(mesh_sum.astype(BF16), lower(3))
    mesh_two = (mesh_one.astype(F32) + finish(3, node_pre_two)).astype(BF16)
    mesh_out_ref[...] = mesh_two
    dec_send[...] = dot(dec_pack_ref[...], mesh_two).astype(BF16)
    dec_table[:own] = mesh_two
    dec_copies = exchange(
        3,
        lambda d: dec_send.at[pl.ds(dec_starts[d], dec_sizes[d])],
        lambda d: dec_table.at[pl.ds(own + dec_starts[d], dec_sizes[d])],
    )

    dec_onehots = [
        onehot_columns(
            columns_of(region_index(dec_source_ref[k], side, DEC_REACH, dec_starts)), n_dec_rows
        )
        for k in range(dec_source_ref.shape[0])
    ]
    for copy in dec_copies:
        copy.wait_recv()
    table = dec_table[...]
    total = grid.astype(F32)
    decode_sum = None
    for onehot in dec_onehots:
        giving_rows = dot(onehot, table).astype(BF16)
        message = finish(4, grid_taking + dot_t(giving_rows, upper(4))).astype(BF16).astype(F32)
        decode_sum = message if decode_sum is None else decode_sum + message
    grid_out_ref[...] = (total + decode_sum).astype(BF16)

    for copies in remote + [halo_copies, sum_copies, mid_copies, dec_copies]:
        for copy in copies:
            copy.wait_send()


def per_device(
    sizes,
    grid_latent,
    mesh_latent,
    w_first,
    first_bias,
    w_second,
    norm_gain,
    encode_source,
    encode_target,
    encode_count,
    mesh_sender,
    mesh_receiver,
    decode_source,
):
    side, _, feat = mesh_latent.shape
    own = side * side
    n_layers = w_first.shape[0]
    enc_matrix, _, enc_sizes = packing(side, ENC_REACH)
    dec_matrix, _, dec_sizes = packing(side, DEC_REACH)
    n_enc, n_dec = sum(enc_sizes), sum(dec_sizes)
    vmem = pl.BlockSpec(memory_space=pltpu.VMEM)
    anywhere = pl.BlockSpec(memory_space=pl.ANY)
    staged = (
        grid_latent,
        mesh_latent.reshape(own, feat),
        first_bias,
        norm_gain,
        encode_source.reshape(1, -1),
        encode_target.reshape(1, -1),
        encode_count.reshape(1, 1),
        mesh_sender.reshape(1, -1),
        mesh_receiver.reshape(1, -1),
        decode_source.transpose(0, 1, 3, 2).reshape(decode_source.shape[3], 1, -1),
        jnp.asarray(enc_matrix, BF16),
        jnp.asarray(enc_matrix.T, BF16),
        jnp.asarray(dec_matrix, BF16),
    )
    grid_out, mesh_out = pl.pallas_call(
        functools.partial(kernel, sizes),
        out_shape=(
            pltpu.VMEM(grid_latent.shape, BF16),
            pltpu.VMEM((own, feat), BF16),
        ),
        in_specs=[anywhere] * (2 + STAGED),
        out_specs=(vmem, vmem),
        scratch_shapes=[pltpu.VMEM(array.shape, array.dtype) for array in staged]
        + [
            pltpu.VMEM((n_layers, feat, 2 * feat), BF16),
            pltpu.VMEM((n_layers, feat, feat), BF16),
            pltpu.VMEM((n_enc, feat), BF16),
            pltpu.VMEM((own + n_enc, feat), BF16),
            pltpu.VMEM((n_enc, feat), BF16),
            pltpu.VMEM((n_enc, feat), BF16),
            pltpu.VMEM((9, own, feat), BF16),
            pltpu.VMEM((n_dec, feat), BF16),
            pltpu.VMEM((own + n_dec, feat), BF16),
            pltpu.SemaphoreType.DMA((STAGED,)),
            pltpu.SemaphoreType.DMA((2, n_layers)),
            pltpu.SemaphoreType.DMA((2, n_layers)),
            pltpu.SemaphoreType.DMA((2, n_layers)),
            pltpu.SemaphoreType.DMA((4, 8)),
            pltpu.SemaphoreType.DMA((4, 8)),
        ],
        compiler_params=pltpu.CompilerParams(
            collective_id=0, has_side_effects=True, vmem_limit_bytes=56 * 1024 * 1024
        ),
    )(w_first.transpose(0, 2, 1), w_second.transpose(0, 2, 1), *staged)
    return grid_out, mesh_out.reshape(mesh_latent.shape)


def solution(mesh):
    sizes = tuple(mesh.shape[name] for name in ("patch", "band", "width"))
    in_specs = (
        P(("groups", "patch", "band", "width"), None),
        P(("groups", "patch"), ("band", "width"), None),
        P(None, None, "width"),
        P(),
        P(None, None, "width"),
        P(),
        P("patch", ("band", "width"), None),
        P("patch", ("band", "width"), None),
        P("patch", ("band", "width")),
        P("patch", ("band", "width"), None),
        P("patch", ("band", "width"), None),
        P("patch", ("band", "width"), None, None),
    )
    out_specs = (
        P(("groups", "patch", "band", "width"), None),
        P(("groups", "patch"), ("band", "width"), None),
    )
    return jax.shard_map(
        functools.partial(per_device, sizes),
        mesh=mesh,
        in_specs=in_specs,
        out_specs=out_specs,
        check_vma=False,
    )
```

```python
import functools

import jax
import jax.numpy as jnp
import numpy as np
from jax import lax
from jax.experimental import pallas as pl
from jax.experimental.pallas import tpu as pltpu
from jax.sharding import PartitionSpec as P

EPSILON = 1e-05
MESH = pl.DeviceIdType.MESH
BF16 = jnp.bfloat16
F32 = jnp.float32
ENC_REACH = 4
DEC_REACH = 1
DIRS = ((1, 0), (-1, 0), (0, 1), (0, -1), (1, 1), (1, -1), (-1, 1), (-1, -1))


def span(step, side, reach):
    if step == 0:
        return list(range(side))
    return list(range(side - reach, side)) if step > 0 else list(range(reach))


def packing(side, reach):
    nodes, starts, sizes = [], [], []
    for dp, dc in DIRS:
        part = [i * side + j for i in span(dp, side, reach) for j in span(dc, side, reach)]
        part = part + [-1] * (-len(part) % 16)
        starts.append(len(nodes))
        sizes.append(len(part))
        nodes.extend(part)
    matrix = np.zeros((len(nodes), side * side), np.float32)
    for place, node in enumerate(nodes):
        if node >= 0:
            matrix[place, node] = 1.0
    return matrix, starts, sizes


def region_index(ext_ids, side, reach, starts):
    ext_side = 3 * side
    own = side * side
    row = (ext_ids * ((1 << 20) // ext_side + 1)) >> 20
    col = ext_ids - ext_side * row
    up, down = row < side, row >= 2 * side
    left, right = col < side, col >= 2 * side
    row_in = row - jnp.where(up, side - reach, jnp.where(down, 2 * side, side))
    col_in = col - jnp.where(left, side - reach, jnp.where(right, 2 * side, side))
    stride = jnp.where(left | right, reach, side)

    def base(dp):
        mid = own + starts[DIRS.index((dp, 0))] if dp else 0
        return jnp.where(
            left,
            own + starts[DIRS.index((dp, 1))],
            jnp.where(right, own + starts[DIRS.index((dp, -1))], mid),
        )

    offset = jnp.where(up, base(1), jnp.where(down, base(-1), base(0)))
    return offset + row_in * stride + col_in


def dot(a, b):
    return jnp.dot(a, b, preferred_element_type=F32)


def dot_t(a, b):
    return lax.dot_general(a, b, (((1,), (1,)), ((), ())), preferred_element_type=F32)


def ones_where(mask):
    return jnp.where(mask, 1.0, 0.0).astype(BF16)


def columns_of(index_row):
    return jnp.transpose(jnp.broadcast_to(index_row, (128, index_row.shape[1])))


def onehot_columns(index_cols, width):
    pieces = []
    for begin in range(0, width, 128):
        size = min(128, width - begin)
        ids = lax.broadcasted_iota(jnp.int32, (index_cols.shape[0], size), 1) + begin
        pieces.append(ones_where(index_cols[:, :size] == ids))
    return pieces[0] if len(pieces) == 1 else jnp.concatenate(pieces, axis=1)


STAGED = 13


def kernel(sizes, *refs):
    w_first_ref, w_second_ref = refs[:2]
    staged_hbm = refs[2 : 2 + STAGED]
    grid_out_ref, mesh_out_ref = refs[2 + STAGED : 4 + STAGED]
    staged = refs[4 + STAGED : 4 + 2 * STAGED]
    (
        grid_ref,
        block_ref,
        bias_ref,
        gain_ref,
        enc_source_ref,
        enc_target_ref,
        enc_count_ref,
        sender_ref,
        receiver_ref,
        dec_source_ref,
        enc_pack_ref,
        enc_unpack_ref,
        dec_pack_ref,
    ) = staged
    (
        full_first,
        full_second,
        enc_send,
        enc_table,
        sum_send,
        sum_recv,
        mid_table,
        dec_send,
        dec_table,
        staged_sem,
        local_sem,
        weight_send_sem,
        weight_recv_sem,
        halo_send_sem,
        halo_recv_sem,
    ) = refs[4 + 2 * STAGED :]
    n_patch, n_band, n_width = sizes
    n_cols = n_band * n_width
    group, patch = lax.axis_index("groups"), lax.axis_index("patch")
    band, core = lax.axis_index("band"), lax.axis_index("width")
    column = band * n_width + core
    n_layers, feat, _ = full_first.shape
    share = w_first_ref.shape[1]
    own_rows = pl.ds(pl.multiple_of(core * share, 16), share)
    own = block_ref.shape[0]
    side = int(round(own**0.5))
    _, enc_starts, enc_sizes = packing(side, ENC_REACH)
    _, dec_starts, dec_sizes = packing(side, DEC_REACH)
    mid_starts = [own * i for i in range(8)]

    def neighbour(dp, dc):
        there = lax.rem(column + dc + n_cols, n_cols)
        return (
            group,
            lax.rem(patch + dp + n_patch, n_patch),
            there // n_width,
            lax.rem(there, n_width),
        )

    partner = (group, patch, band, 1 - core)

    barrier = pltpu.get_barrier_semaphore()
    for dp, dc in DIRS:
        pl.semaphore_signal(barrier, inc=1, device_id=neighbour(dp, dc), device_id_type=MESH)

    staging = []
    for i in range(STAGED):
        copy = pltpu.make_async_copy(staged_hbm[i], staged[i], staged_sem.at[i])
        copy.start()
        staging.append(copy)
    local = []
    for k in range(n_layers):
        pair = []
        for s, (src, dst) in enumerate(((w_first_ref, full_first), (w_second_ref, full_second))):
            copy = pltpu.make_async_copy(src.at[k], dst.at[k, own_rows], local_sem.at[s, k])
            copy.start()
            pair.append(copy)
        local.append(pair)

    for copy in staging:
        copy.wait()
    block = block_ref[...]
    enc_send[...] = dot(enc_pack_ref[...], block).astype(BF16)
    enc_table[:own] = block
    pl.semaphore_wait(barrier, len(DIRS))

    def exchange(phase, source_of, target_of, towards=1, chosen=None):
        copies = []
        for d in (0, 1, 4, 5, 6, 7, 2, 3) if chosen is None else chosen:
            dp, dc = DIRS[d][0], DIRS[d][1]
            if chosen and len(chosen) < 4:
                dp = 0
            copy = pltpu.make_async_remote_copy(
                src_ref=source_of(d),
                dst_ref=target_of(d),
                send_sem=halo_send_sem.at[phase, d],
                recv_sem=halo_recv_sem.at[phase, d],
                device_id=neighbour(towards * dp, towards * dc),
                device_id_type=MESH,
            )
            copy.start()
            copies.append(copy)
        return copies

    halo_copies = exchange(
        0,
        lambda d: enc_send.at[pl.ds(enc_starts[d], enc_sizes[d])],
        lambda d: enc_table.at[pl.ds(own + enc_starts[d], enc_sizes[d])],
    )
    remote = []
    for k in range(n_layers):
        pair = []
        for s, (src, dst) in enumerate(((w_first_ref, full_first), (w_second_ref, full_second))):
            copy = pltpu.make_async_remote_copy(
                src_ref=src.at[k],
                dst_ref=dst.at[k, own_rows],
                send_sem=weight_send_sem.at[s, k],
                recv_sem=weight_recv_sem.at[s, k],
                device_id=partner,
                device_id_type=MESH,
            )
            copy.start()
            pair.append(copy)
        remote.append(pair)

    def take_weights(k):
        for s in range(2):
            local[k][s].wait()
            remote[k][s].wait_recv()

    def upper(k):
        return full_first[k, :, :feat]

    def lower(k):
        return full_first[k, :, feat:]

    def finish(k, summed):
        half = 0.5 * summed
        hidden = (half + half * jnp.tanh(half)).astype(BF16)
        result = dot_t(hidden, full_second[k])
        centre = jnp.mean(result, axis=-1, keepdims=True)
        shifted = result - centre
        variance = jnp.mean(shifted * shifted, axis=-1, keepdims=True)
        return shifted * lax.rsqrt(variance + EPSILON) * gain_ref[k : k + 1, :]

    def bias(k):
        return bias_ref[k : k + 1, :]

    grid = grid_ref[...]
    n_grid = grid.shape[0]
    n_enc = enc_target_ref.shape[1]
    own_enc = min(n_grid, n_enc)
    source_cols = columns_of(enc_source_ref[...][:, own_enc:])
    more = dot(onehot_columns(source_cols, n_grid), grid).astype(BF16)
    sending = jnp.concatenate([grid, more], axis=0)
    n_enc_rows = own + sum(enc_sizes)
    target_row = region_index(enc_target_ref[...], side, ENC_REACH, enc_starts)
    target_onehot = onehot_columns(columns_of(target_row), n_enc_rows)
    slot_ids = lax.broadcasted_iota(jnp.int32, (1, n_enc), 1)
    kept_row = jnp.where(slot_ids < enc_count_ref[...], target_row, -1)
    node_ids = lax.broadcasted_iota(jnp.int32, (n_enc_rows, n_enc), 0)
    scatter = ones_where(node_ids == kept_row)
    take_weights(0)
    grid_term = dot_t(sending, upper(0)) + bias(0)
    for copy in halo_copies:
        copy.wait_recv()
    target_rows = dot(target_onehot, enc_table[...]).astype(BF16)
    messages = finish(0, grid_term + dot_t(target_rows, lower(0))).astype(BF16)
    sum_send[...] = dot(scatter[own:], messages).astype(BF16)
    sum_copies = exchange(
        1,
        lambda d: sum_send.at[pl.ds(enc_starts[d], enc_sizes[d])],
        lambda d: sum_recv.at[pl.ds(enc_starts[d], enc_sizes[d])],
        -1,
    )

    own_partial = dot(scatter[:own], messages)

    take_weights(1)
    node_term = dot_t(block, upper(1)) + bias(1)
    take_weights(2)
    take_weights(3)
    for copy in sum_copies:
        copy.wait_recv()
    encode_sum = own_partial + dot(enc_unpack_ref[...], sum_recv[...])
    node_pre = node_term + dot_t(encode_sum.astype(BF16), lower(1))
    mesh_one = (block.astype(F32) + finish(1, node_pre)).astype(BF16)
    mid_table[0] = mesh_one
    mid_copies = exchange(
        2, lambda d: mid_table.at[0], lambda d: mid_table.at[1 + d], 1, (0, 1, 2, 3)
    )

    receiver_row = receiver_ref[...]
    n_edges = receiver_row.shape[1]
    taking_rows = dot(onehot_columns(columns_of(receiver_row), own), mesh_one).astype(BF16)
    edge_term = dot_t(taking_rows, lower(2)) + bias(2)
    for d in range(2):
        mid_copies[d].wait_recv()
        corners = (4 + 2 * d, 5 + 2 * d)
        mid_copies = mid_copies + exchange(
            2, lambda c: mid_table.at[1 + d], lambda c: mid_table.at[1 + c], 1, corners
        )
    own_ids = lax.broadcasted_iota(jnp.int32, (own, n_edges), 0)
    edge_scatter = ones_where(own_ids == receiver_row)
    sender_row = region_index(sender_ref[...], side, side, mid_starts)
    sender_cols = columns_of(sender_row)
    sender_near = onehot_columns(sender_cols, 5 * own)
    sender_far = onehot_columns(sender_cols - 5 * own, 4 * own)
    node_term_two = dot_t(mesh_one, upper(3)) + bias(3)
    take_weights(4)
    grid_taking = dot_t(grid, lower(4)) + bias(4)
    n_dec_rows = own + sum(dec_sizes)
    for copy in mid_copies[2:4]:
        copy.wait_recv()
    sending_rows = dot(sender_near, mid_table[:5].reshape(5 * own, feat))
    for copy in mid_copies[4:]:
        copy.wait_recv()
    sending_rows = sending_rows + dot(
        sender_far, mid_table[5:].reshape(4 * own, feat)
    )
    sending_rows = sending_rows.astype(BF16)
    edge_messages = finish(2, edge_term + dot_t(sending_rows, upper(2))).astype(BF16)
    mesh_sum = dot(edge_scatter, edge_messages)
    node_pre_two = node_term_two + dot_t(mesh_sum.astype(BF16), lower(3))
    mesh_two = (mesh_one.astype(F32) + finish(3, node_pre_two)).astype(BF16)
    mesh_out_ref[...] = mesh_two
    dec_send[...] = dot(dec_pack_ref[...], mesh_two).astype(BF16)
    dec_table[:own] = mesh_two
    dec_copies = exchange(
        3,
        lambda d: dec_send.at[pl.ds(dec_starts[d], dec_sizes[d])],
        lambda d: dec_table.at[pl.ds(own + dec_starts[d], dec_sizes[d])],
    )

    dec_onehots = [
        onehot_columns(
            columns_of(region_index(dec_source_ref[k], side, DEC_REACH, dec_starts)), n_dec_rows
        )
        for k in range(dec_source_ref.shape[0])
    ]
    for copy in dec_copies:
        copy.wait_recv()
    table = dec_table[...]
    total = grid.astype(F32)
    degree = len(dec_onehots)
    giving_rows = dot(jnp.concatenate(dec_onehots, axis=0), table).astype(BF16)
    taking = jnp.concatenate([grid_taking] * degree, axis=0)
    messages = finish(4, taking + dot_t(giving_rows, upper(4))).astype(BF16).astype(F32)
    decode_sum = jnp.sum(messages.reshape(degree, n_grid, feat), axis=0)
    grid_out_ref[...] = (total + decode_sum).astype(BF16)

    for copies in remote + [halo_copies, sum_copies, mid_copies, dec_copies]:
        for copy in copies:
            copy.wait_send()


def per_device(
    sizes,
    grid_latent,
    mesh_latent,
    w_first,
    first_bias,
    w_second,
    norm_gain,
    encode_source,
    encode_target,
    encode_count,
    mesh_sender,
    mesh_receiver,
    decode_source,
):
    side, _, feat = mesh_latent.shape
    own = side * side
    n_layers = w_first.shape[0]
    enc_matrix, _, enc_sizes = packing(side, ENC_REACH)
    dec_matrix, _, dec_sizes = packing(side, DEC_REACH)
    n_enc, n_dec = sum(enc_sizes), sum(dec_sizes)
    vmem = pl.BlockSpec(memory_space=pltpu.VMEM)
    anywhere = pl.BlockSpec(memory_space=pl.ANY)
    staged = (
        grid_latent,
        mesh_latent.reshape(own, feat),
        first_bias,
        norm_gain,
        encode_source.reshape(1, -1),
        encode_target.reshape(1, -1),
        encode_count.reshape(1, 1),
        mesh_sender.reshape(1, -1),
        mesh_receiver.reshape(1, -1),
        decode_source.transpose(0, 1, 3, 2).reshape(decode_source.shape[3], 1, -1),
        jnp.asarray(enc_matrix, BF16),
        jnp.asarray(enc_matrix.T, BF16),
        jnp.asarray(dec_matrix, BF16),
    )
    grid_out, mesh_out = pl.pallas_call(
        functools.partial(kernel, sizes),
        out_shape=(
            pltpu.VMEM(grid_latent.shape, BF16),
            pltpu.VMEM((own, feat), BF16),
        ),
        in_specs=[anywhere] * (2 + STAGED),
        out_specs=(vmem, vmem),
        scratch_shapes=[pltpu.VMEM(array.shape, array.dtype) for array in staged]
        + [
            pltpu.VMEM((n_layers, feat, 2 * feat), BF16),
            pltpu.VMEM((n_layers, feat, feat), BF16),
            pltpu.VMEM((n_enc, feat), BF16),
            pltpu.VMEM((own + n_enc, feat), BF16),
            pltpu.VMEM((n_enc, feat), BF16),
            pltpu.VMEM((n_enc, feat), BF16),
            pltpu.VMEM((9, own, feat), BF16),
            pltpu.VMEM((n_dec, feat), BF16),
            pltpu.VMEM((own + n_dec, feat), BF16),
            pltpu.SemaphoreType.DMA((STAGED,)),
            pltpu.SemaphoreType.DMA((2, n_layers)),
            pltpu.SemaphoreType.DMA((2, n_layers)),
            pltpu.SemaphoreType.DMA((2, n_layers)),
            pltpu.SemaphoreType.DMA((4, 8)),
            pltpu.SemaphoreType.DMA((4, 8)),
        ],
        compiler_params=pltpu.CompilerParams(
            collective_id=0, has_side_effects=True, vmem_limit_bytes=56 * 1024 * 1024
        ),
    )(w_first.transpose(0, 2, 1), w_second.transpose(0, 2, 1), *staged)
    return grid_out, mesh_out.reshape(mesh_latent.shape)


def solution(mesh):
    sizes = tuple(mesh.shape[name] for name in ("patch", "band", "width"))
    in_specs = (
        P(("groups", "patch", "band", "width"), None),
        P(("groups", "patch"), ("band", "width"), None),
        P(None, None, "width"),
        P(),
        P(None, None, "width"),
        P(),
        P("patch", ("band", "width"), None),
        P("patch", ("band", "width"), None),
        P("patch", ("band", "width")),
        P("patch", ("band", "width"), None),
        P("patch", ("band", "width"), None),
        P("patch", ("band", "width"), None, None),
    )
    out_specs = (
        P(("groups", "patch", "band", "width"), None),
        P(("groups", "patch"), ("band", "width"), None),
    )
    return jax.shard_map(
        functools.partial(per_device, sizes),
        mesh=mesh,
        in_specs=in_specs,
        out_specs=out_specs,
        check_vma=False,
    )
```
